32 devices in a mesh: wide: 8 (over y, x, core), narrow: 4 (over z).
Axes of the slice: x: 2, y: 2, z: 4, core: 2. Of those that a mesh axis runs over, the one named last changes fastest.
Arguments:
- old_field: float32 [1024, 128, 128], P(('wide', 'narrow')), may hold values from -6 to 6
- old_level: int32 [1024], P(('wide', 'narrow')), may hold values from 0 to 1
- new_source: int32 [16, 16], P('wide', 'narrow'), may hold values from 0 to 1023, as said below
- stretch_coef: float32 [4096, 4096], P('wide', 'narrow'), may hold values from 0.2 to 2
- bend_coef: float32 [4096, 4096], P('wide', 'narrow'), may hold values from 0.05 to 0.5
- load_field: float32 [4096, 4096], P('wide', 'narrow'), may hold values from -6 to 6
Outputs:
- relaxed: float32 [4096, 4096], P('wide', 'narrow')
The draws below stay inside these ranges and needn't reach their ends.
Inputs may be any that keep to these rules, and one draw needn't show every extreme that they name: new_source names an old block held by a device with the same narrow index; one old device gives at most 2 sibling groups to one new device, and exactly 2 wherever it gives any.
All inputs are finite; a program needn't handle non-finite values.
Results may differ from the reference program's by a relative error of at most 0.0001.
Values sent between devices are 32-bit elements; how exact they have to be, the bound alone decides.
A program may use at most 128 MiB of HBM per device.

```python
import math
import jax
import jax.numpy as jnp
from jax import lax

BS = 128
BX_DEV = 4
BY_DEV = 8
SWEEPS = 2
BLK_DEV = 32
RANKS = 8
SEGS = 4
CAP = 2
NOLD = 1024
NGX = 16
NGY = 16
NX = 4096
NY = 4096


def draw_new_source(key, part):
    group_rows = BX_DEV // 2
    group_cols = BY_DEV // 2
    group_x = jnp.arange(NGX, dtype=jnp.int32)[:, None]
    group_y = jnp.arange(NGY, dtype=jnp.int32)[None, :]
    rank_w = group_x // group_rows
    seg_n = group_y // group_cols
    local_k = group_x % group_rows * group_cols + group_y % group_cols
    group_id = local_k // CAP
    scores = jax.random.randint(jax.random.fold_in(key, 12), (RANKS, SEGS, RANKS), 0, 1 << 20, dtype=jnp.int32)
    scores = scores * RANKS + jnp.arange(RANKS, dtype=jnp.int32)[None, None, :]
    shuffle = jnp.argsort(scores, axis=-1, stable=True).astype(jnp.int32)
    offset = shuffle[rank_w, seg_n, group_id]
    from_rank = (rank_w + offset) % RANKS
    from_local = jax.random.randint(jax.random.fold_in(key, 13), (NGX, NGY), 0, BLK_DEV, dtype=jnp.int32)
    return ((from_rank * SEGS + seg_n) * BLK_DEV + from_local).astype(jnp.int32)


def touch_ends(array, own_key, least, high):
    index_at = [jax.random.randint(jax.random.fold_in(own_key, axis), (), 0, length) for axis, length in enumerate(array.shape)]
    widest = array.shape.index(max(array.shape))
    beside = index_at[:widest] + [(index_at[widest] + 1) % array.shape[widest]] + index_at[widest + 1:]
    return array.at[tuple(index_at)].set(least).at[tuple(beside)].set(high)


def shard_levels(stream_key, extent, pieces, smallest, top_value):
    level = 1.0
    for dim, parts in pieces:
        draws = jax.random.uniform(jax.random.fold_in(jax.random.fold_in(stream_key, 6), dim), (parts,), jnp.float32, smallest / len(pieces), top_value / len(pieces))
        level = level * jnp.repeat(jnp.exp(draws), extent[dim] // parts).reshape((-1,) + (1,) * (len(extent) - 1 - dim))
    return level


def gaussian(stream_key, shape, scale, reach, shards=(), kind=jnp.bfloat16):
    result = scale * jax.random.normal(stream_key, shape, jnp.float32)
    if shards:
        result = result * shard_levels(stream_key, shape, shards, -0.22, 0.18)
    return jnp.clip(result, -reach, reach).astype(kind)


def setup_inputs(seed: int = 0) -> dict:
    seeds = jax.random.split(jax.random.key(seed), 7)
    return {
        "old_field": gaussian(seeds[0], (NOLD, BS, BS), 1.0, 6.0, ((0, 32),), jnp.float32),
        "old_level": touch_ends(jax.random.randint(seeds[1], (NOLD,), 0, 2), jax.random.fold_in(seeds[1], 1), 0, 1).astype(jnp.int32),
        "new_source": draw_new_source(jax.random.fold_in(seeds[6], 71), 0),
        "stretch_coef": jnp.clip(jnp.exp(math.log(2.0) - 2.3025851 * jax.random.uniform(seeds[3], (NX, NY), jnp.float32) ** shard_levels(seeds[3], (NX, NY), ((0, 8), (1, 4)), -0.2, 0.2)), 0.2, 2.0),
        "bend_coef": jnp.clip(jnp.exp(math.log(0.5) - 2.3025851 * jax.random.uniform(seeds[4], (NX, NY), jnp.float32) ** shard_levels(seeds[4], (NX, NY), ((0, 8), (1, 4)), -0.2, 0.2)), 0.05, 0.5),
        "load_field": gaussian(seeds[5], (NX, NY), 1.0, 6.0, ((0, 8), (1, 4)), jnp.float32),
    }


OMEGA = 0.5


def quadrant_table(side_cells, half_index):
    half_size = side_cells // 2
    row_ids = jnp.arange(side_cells, dtype=jnp.int32)[:, None]
    col_ids = jnp.arange(side_cells, dtype=jnp.int32)[None, :]
    base_cell = half_index * half_size
    near_cell = base_cell + row_ids // 2
    other_cell = near_cell + jnp.where(row_ids % 2 == 1, 1, -1)
    other_cell = jnp.clip(other_cell, base_cell, base_cell + half_size - 1)
    return 0.75 * (col_ids == near_cell).astype(jnp.float32) + 0.25 * (col_ids == other_cell).astype(jnp.float32)


def refine_group(parents):
    side_cells = parents.shape[-1]
    tables = [quadrant_table(side_cells, 0), quadrant_table(side_cells, 1)]
    upper = [jnp.einsum("ij,njk->nik", table, parents, precision=lax.Precision.HIGHEST) for table in tables]
    rows_out = []
    for half_x in range(2):
        pair = [jnp.einsum("nik,lk->nil", upper[half_x], tables[half_y], precision=lax.Precision.HIGHEST) for half_y in range(2)]
        rows_out.append(jnp.stack(pair, axis=1))
    return jnp.stack(rows_out, axis=1)


def spacing_factor(levels):
    return 1.0 + 3.0 * (levels >= 1).astype(jnp.float32)


def relax(field_pad, stretch_pad, bend_pad, load_core, inside):
    center = field_pad[2:-2, 2:-2]
    laplace = field_pad[:-2, 1:-1] + field_pad[2:, 1:-1] + field_pad[1:-1, :-2] + field_pad[1:-1, 2:] - 4.0 * field_pad[1:-1, 1:-1]
    moment = bend_pad * laplace
    bending = moment[:-2, 1:-1] + moment[2:, 1:-1] + moment[1:-1, :-2] + moment[1:-1, 2:] - 4.0 * moment[1:-1, 1:-1]
    stretch_mid = stretch_pad[1:-1, 1:-1]
    diagonal = 16.0 * bend_pad[1:-1, 1:-1]
    stretching = jnp.zeros_like(center)
    neighbours = (
        (stretch_pad[:-2, 1:-1], bend_pad[:-2, 1:-1], field_pad[1:-3, 2:-2]),
        (stretch_pad[2:, 1:-1], bend_pad[2:, 1:-1], field_pad[3:-1, 2:-2]),
        (stretch_pad[1:-1, :-2], bend_pad[1:-1, :-2], field_pad[2:-2, 1:-3]),
        (stretch_pad[1:-1, 2:], bend_pad[1:-1, 2:], field_pad[2:-2, 3:-1]),
    )
    for near_stretch, near_bend, near_field in neighbours:
        face_coef = 0.5 * (stretch_mid + near_stretch)
        stretching = stretching + face_coef * (center - near_field)
        diagonal = diagonal + face_coef + near_bend
    remainder = load_core - (stretching + bending)
    if inside is None:
        return center + OMEGA * remainder / diagonal
    safe_diag = jnp.where(inside, diagonal, 1.0)
    return jnp.where(inside, center + OMEGA * remainder / safe_diag, 0.0)


def reference(old_field, old_level, new_source, stretch_coef, bend_coef, load_field):
    flat_source = new_source.reshape(-1)
    children = refine_group(old_field[flat_source])
    spacing = spacing_factor(old_level[flat_source])
    grid_field = children.reshape(NGX, NGY, 2, 2, BS, BS).transpose(0, 2, 4, 1, 3, 5).reshape(NX, NY)
    scale_grid = jnp.repeat(jnp.repeat(spacing.reshape(NGX, NGY), 2 * BS, axis=0), 2 * BS, axis=1)
    stretch_eff = stretch_coef * scale_grid
    bend_eff = bend_coef * scale_grid * scale_grid
    stretch_pad = jnp.pad(stretch_eff, 1)
    bend_pad = jnp.pad(bend_eff, 1)
    for sweep_index in range(SWEEPS):
        grid_field = relax(jnp.pad(grid_field, 2), stretch_pad, bend_pad, load_field, None)
    return grid_field
```

```python
import functools

import jax
import jax.numpy as jnp
from jax import lax
from jax.experimental import pallas as pl
from jax.experimental.pallas import tpu as pltpu
from jax.sharding import PartitionSpec as P

SWEEPS = 2
OMEGA = 0.5
CAPACITY = 2
LANES = 128
EDGE = 16
HALO = 8
STEP = 16
SLOT = 8
PIECES = 4
MESH = pl.DeviceIdType.MESH


def refine_table(half, rows, cols):
    side = 2 * half
    base = jnp.where(rows >= side, half, 0)
    inner = jnp.where(rows >= side, rows - side, rows)
    near = base + (inner >> 1)
    other = near + jnp.where((inner & 1) == 1, 1, -1)
    other = jnp.minimum(jnp.maximum(other, base), base + half - 1)
    return jnp.where(cols == near, 0.75, 0.0) + jnp.where(cols == other, 0.25, 0.0)


def split3(x):
    high = x.astype(jnp.bfloat16)
    rest = x - high.astype(jnp.float32)
    mid = rest.astype(jnp.bfloat16)
    low = (rest - mid.astype(jnp.float32)).astype(jnp.bfloat16)
    return high, mid, low


def laplace(big):
    total, width = big.shape
    rows = total - 2 * HALO
    center = big[HALO : HALO + rows]
    above = pltpu.roll(big, 1, 0)[HALO : HALO + rows]
    below = pltpu.roll(big, total - 1, 0)[HALO : HALO + rows]
    left = pltpu.roll(center, 1, 1)
    right = pltpu.roll(center, width - 1, 1)
    return (above + below) + (left + right) - 4.0 * center, center


def kernel(
    wide_count, narrow_count, groups_x, groups_y,
    msg, old_hbm, stretch_hbm, bend_hbm, load_hbm, out_hbm,
    old, table, table_s, send, recv, grid, lap_u, weight, moment, rest, pack, unpacked, corner,
    table_row, table_col, result,
    load_sem, table_send, table_recv, smem_sem, par_send, par_recv, halo_send, halo_recv, out_sem,
):
    me = lax.axis_index("wide")
    seg = lax.axis_index("narrow")
    per_device, side, _ = old.shape
    per_groups = groups_x * groups_y
    span = 2 * side
    rows, cols = groups_x * span, groups_y * span
    width = cols + LANES
    chunk = rows * SLOT // LANES
    has_up, has_down = me > 0, me < wide_count - 1
    has_left, has_right = seg > 0, seg < narrow_count - 1
    up, down = lax.rem(me + wide_count - 1, wide_count), lax.rem(me + 1, wide_count)
    left, right = lax.rem(seg + narrow_count - 1, narrow_count), lax.rem(seg + 1, narrow_count)

    tile_rows = pl.ds(EDGE, rows)
    loads = [
        pltpu.make_async_copy(old_hbm, old, load_sem.at[0]),
        pltpu.make_async_copy(stretch_hbm, grid.at[0, tile_rows, pl.ds(0, cols)], load_sem.at[1]),
        pltpu.make_async_copy(bend_hbm, grid.at[1, tile_rows, pl.ds(0, cols)], load_sem.at[2]),
        pltpu.make_async_copy(load_hbm, grid.at[2, tile_rows, pl.ds(0, cols)], load_sem.at[3]),
    ]
    for copy in loads:
        copy.start()

    peers = [(lax.rem(me + k, wide_count), seg) for k in range(1, wide_count)]
    peers += [(me, left), (me, right), (up, left), (up, right), (down, left), (down, right)]
    barrier = pltpu.get_barrier_semaphore()
    for peer in peers:
        pl.semaphore_signal(barrier, inc=1, device_id=peer, device_id_type=MESH)
    pl.semaphore_wait(barrier, len(peers))

    table_copies = []
    for k in range(1, wide_count):
        copy = pltpu.make_async_remote_copy(
            src_ref=msg, dst_ref=table.at[me], send_sem=table_send.at[k], recv_sem=table_recv.at[k],
            device_id=(lax.rem(me + k, wide_count), seg), device_id_type=MESH,
        )
        copy.start()
        table_copies.append(copy)
    table[me] = msg[...]

    half = side // 2
    shape = (span, side)
    by_row = refine_table(
        half, lax.broadcasted_iota(jnp.int32, shape, 0), lax.broadcasted_iota(jnp.int32, shape, 1)
    ).astype(jnp.bfloat16)
    shape = (side, span)
    by_col = refine_table(
        half, lax.broadcasted_iota(jnp.int32, shape, 1), lax.broadcasted_iota(jnp.int32, shape, 0)
    ).astype(jnp.bfloat16)
    for part in range(3):
        table_row[:, part * side : (part + 1) * side] = by_row
        table_col[part * side : (part + 1) * side, :] = by_col

    for copy in table_copies:
        copy.wait()
    to_smem = pltpu.make_async_copy(table, table_s, smem_sem)
    to_smem.start()
    to_smem.wait()

    loads[0].wait()
    block = per_device * narrow_count

    def picks(dest):
        first, second, seen = jnp.int32(0), jnp.int32(0), jnp.int32(0)
        for j in range(per_groups):
            source = table_s[dest, 0, j]
            mine = lax.div(source, jnp.int32(block)) == me
            where = lax.rem(source, jnp.int32(per_device))
            first = jnp.where(mine & (seen == 0), where, first)
            second = jnp.where(mine & (seen == 1), where, second)
            seen = seen + mine.astype(jnp.int32)
        return first, second

    parent_copies = []
    for k in range(1, wide_count):
        dest = lax.rem(me + k, wide_count)
        first, second = picks(dest)
        send[k, 0] = old[first]
        send[k, 1] = old[second]
        copy = pltpu.make_async_remote_copy(
            src_ref=send.at[k], dst_ref=recv.at[me], send_sem=par_send.at[k], recv_sem=par_recv.at[k],
            device_id=(dest, seg), device_id_type=MESH,
        )
        copy.start()
        parent_copies.append(copy)
    first, second = picks(me)
    recv[me, 0] = old[first]
    recv[me, 1] = old[second]

    ranks = []
    places = []
    for j in range(per_groups):
        source = table_s[me, 0, j]
        rank = lax.div(source, jnp.int32(block))
        slot = jnp.int32(0)
        for earlier in ranks:
            slot = slot + (earlier == rank).astype(jnp.int32)
        ranks.append(rank)
        places.append((rank, jnp.minimum(slot, CAPACITY - 1)))
    loads[1].wait()
    loads[2].wait()
    loads[3].wait()
    for j in range(per_groups):
        source = table_s[me, 0, j]
        level = table_s[ranks[j], 0, per_groups + lax.rem(source, jnp.int32(per_device))]
        factor = jnp.where(level >= 1, 4.0, 1.0).astype(jnp.float32)
        at_row = EDGE + j // groups_y * span
        at_col = j % groups_y * span

        @pl.loop(0, span // 32)
        def _(i):
            here = pl.ds(pl.multiple_of(at_row + i * 32, 8), 32)
            there = pl.ds(at_col, span)
            grid[0, here, there] = grid[0, here, there] * (0.5 * factor)
            grid[1, here, there] = grid[1, here, there] * (factor * factor)

    lane = lax.broadcasted_iota(jnp.int32, (chunk, LANES), 1)

    def exchange(first_plane, planes, phase):
        picked = pl.ds(first_plane, planes)
        for plane in range(first_plane, first_plane + planes):
            to_left = jnp.zeros((chunk, LANES), jnp.float32)
            to_right = to_left
            for i in range(LANES // SLOT):
                here = pl.ds(EDGE + i * chunk, chunk)
                mine = (lane >= i * SLOT) & (lane < (i + 1) * SLOT)
                head = grid[plane, here, 0:LANES]
                tail = grid[plane, here, cols - LANES : cols]
                if i:
                    head = pltpu.roll(head, i * SLOT, 1)
                if (i + 1) * SLOT < LANES:
                    tail = pltpu.roll(tail, (i + 1) * SLOT, 1)
                to_left = jnp.where(mine, head, to_left)
                to_right = jnp.where(mine, tail, to_right)
            pack[0, plane] = to_left
            pack[1, plane] = to_right
        top, bottom = pl.ds(EDGE, HALO), pl.ds(EDGE + rows - HALO, HALO)
        over, under = pl.ds(EDGE - HALO, HALO), pl.ds(EDGE + rows, HALO)
        every = pl.ds(0, cols)
        first, last = pl.ds(0, LANES), pl.ds(cols - LANES, LANES)
        plan = [
            (grid.at[picked, top, every], grid.at[picked, under, every], (up, seg)),
            (grid.at[picked, bottom, every], grid.at[picked, over, every], (down, seg)),
            (pack.at[0, picked], unpacked.at[0, picked], (me, left)),
            (pack.at[1, picked], unpacked.at[1, picked], (me, right)),
            (grid.at[picked, top, first], corner.at[0, picked], (up, left)),
            (grid.at[picked, top, last], corner.at[1, picked], (up, right)),
            (grid.at[picked, bottom, first], corner.at[2, picked], (down, left)),
            (grid.at[picked, bottom, last], corner.at[3, picked], (down, right)),
        ]
        copies = []
        for i, (source, target, device) in enumerate(plan):
            copy = pltpu.make_async_remote_copy(
                src_ref=source, dst_ref=target,
                send_sem=halo_send.at[phase, i], recv_sem=halo_recv.at[phase, i],
                device_id=device, device_id_type=MESH,
            )
            copy.start()
            copies.append(copy)
        return copies

    edge_lane = lax.broadcasted_iota(jnp.int32, (HALO, LANES), 1)

    def settle(copies, first_plane, planes):
        for copy in copies:
            copy.wait()
        beside = pl.ds(cols, LANES)
        for plane in range(first_plane, first_plane + planes):
            from_right, from_left = unpacked[0, plane], unpacked[1, plane]
            inside = jnp.where(lane < LANES // 2, has_right.astype(jnp.int32), has_left.astype(jnp.int32)) > 0
            for i in range(LANES // SLOT):
                head, tail = from_right, from_left
                if i:
                    head = pltpu.roll(head, LANES - i * SLOT, 1)
                if (i + 1) * SLOT < LANES:
                    tail = pltpu.roll(tail, LANES - (i + 1) * SLOT, 1)
                joined = jnp.where(lane < LANES // 2, head, tail)
                grid[plane, pl.ds(EDGE + i * chunk, chunk), beside] = jnp.where(inside, joined, 0.0)
            for at, is_there, pair in ((EDGE + rows, has_down, 0), (EDGE - HALO, has_up, 2)):
                here = pl.ds(at, HALO)
                joined = jnp.where(edge_lane < LANES // 2, corner[pair, plane], corner[pair + 1, plane])
                keep = jnp.where(
                    edge_lane < LANES // 2, has_right.astype(jnp.int32), has_left.astype(jnp.int32)
                ) * is_there.astype(jnp.int32)
                grid[plane, here, beside] = jnp.where(keep > 0, joined, 0.0)
                every = grid[plane, here, 0:cols]
                grid[plane, here, 0:cols] = jnp.where(is_there, every, jnp.zeros_like(every))

    def clear_outside():
        beside = pl.ds(cols, LANES)
        total = rows + 2 * HALO
        inside_lane = lax.broadcasted_iota(jnp.int32, (total, LANES), 1)
        keep = jnp.where(inside_lane < LANES // 2, has_right.astype(jnp.int32), has_left.astype(jnp.int32)) > 0
        here = pl.ds(EDGE - HALO, total)
        grid[3, here, beside] = jnp.where(keep, grid[3, here, beside], 0.0)
        for at, is_there in ((EDGE + rows, has_down), (EDGE - HALO, has_up)):
            here = pl.ds(at, HALO)
            every = grid[3, here, :]
            grid[3, here, :] = jnp.where(is_there, every, jnp.zeros_like(every))

    steps = (rows + 2 * HALO) // STEP

    def window(i, start):
        at = start + i * STEP
        return pl.ds(pl.multiple_of(at - HALO, 8), STEP + 2 * HALO), pl.ds(pl.multiple_of(at, 8), STEP)

    settle(exchange(0, 3, 0), 0, 3)

    @pl.loop(0, steps)
    def _(i):
        around, here = window(i, EDGE - HALO)
        of_u, mid_u = laplace(grid[0, around, :])
        of_b, mid_b = laplace(grid[1, around, :])
        lap_u[here, :] = of_u
        weight[here, :] = OMEGA / (of_u + of_b + 8.0 * mid_u + 20.0 * mid_b)

    for copy in parent_copies:
        copy.wait()
    for j in range(per_groups):
        rank, slot = places[j]
        parent = recv[rank, slot]
        wider = jnp.dot(
            jnp.concatenate(split3(parent), axis=1), table_col[...], preferred_element_type=jnp.float32
        )
        child = jnp.dot(
            table_row[...], jnp.concatenate(split3(wider), axis=0), preferred_element_type=jnp.float32
        )
        grid[3, pl.ds(EDGE + j // groups_y * span, span), pl.ds(j % groups_y * span, span)] = child

    settle(exchange(3, 1, 1), 3, 1)

    def first_half():
        @pl.loop(0, steps)
        def _(i):
            around, here = window(i, EDGE - HALO)
            of_v, mid = laplace(grid[3, around, :])
            coef = grid[0, here, :]
            moment[here, :] = grid[1, here, :] * of_v - coef * mid
            rest[here, :] = grid[2, here, :] - (mid * lap_u[here, :] - coef * of_v)

    def second_half(i, start):
        around, here = window(i, start)
        of_m, _ = laplace(moment[around, :])
        return here, grid[3, here, :] + weight[here, :] * (rest[here, :] - of_m)

    for sweep in range(SWEEPS - 1):
        first_half()

        @pl.loop(0, steps)
        def _(i):
            here, value = second_half(i, EDGE - HALO)
            grid[3, here, :] = value

        clear_outside()

    first_half()
    piece = rows // PIECES
    stores = []
    for p in range(PIECES):

        @pl.loop(0, piece // STEP)
        def _(i):
            _, value = second_half(i, EDGE + p * piece)
            result[pl.ds(pl.multiple_of(p * piece + i * STEP, 8), STEP), :] = value[:, 0:cols]

        part = pl.ds(p * piece, piece)
        copy = pltpu.make_async_copy(result.at[part, :], out_hbm.at[part, :], out_sem.at[p])
        copy.start()
        stores.append(copy)
    for copy in stores:
        copy.wait()


def local(old_field, old_level, new_source, stretch_coef, bend_coef, load_field):
    wide_count = lax.axis_size("wide")
    narrow_count = lax.axis_size("narrow")
    groups_x, groups_y = new_source.shape
    per_device, side, _ = old_field.shape
    rows, cols = stretch_coef.shape
    used = groups_x * groups_y + per_device
    length = -(-used // LANES) * LANES
    msg = jnp.concatenate(
        [new_source.reshape(-1), old_level, jnp.zeros((length - used,), jnp.int32)]
    ).reshape(1, length)
    full = (rows + 2 * EDGE, cols + LANES)
    chunk = rows * SLOT // LANES
    span = 2 * side
    f32 = jnp.float32
    dma = pltpu.SemaphoreType.DMA
    return pl.pallas_call(
        functools.partial(kernel, wide_count, narrow_count, groups_x, groups_y),
        out_shape=jax.ShapeDtypeStruct((rows, cols), f32),
        in_specs=[pl.BlockSpec(memory_space=pltpu.VMEM)] + [pl.BlockSpec(memory_space=pl.ANY)] * 4,
        out_specs=pl.BlockSpec(memory_space=pl.ANY),
        scratch_shapes=[
            pltpu.VMEM(old_field.shape, f32),
            pltpu.VMEM((wide_count, 1, length), jnp.int32),
            pltpu.SMEM((wide_count, 1, length), jnp.int32),
            pltpu.VMEM((wide_count, CAPACITY, side, side), f32),
            pltpu.VMEM((wide_count, CAPACITY, side, side), f32),
            pltpu.VMEM((4,) + full, f32),
            pltpu.VMEM(full, f32),
            pltpu.VMEM(full, f32),
            pltpu.VMEM(full, f32),
            pltpu.VMEM(full, f32),
            pltpu.VMEM((2, 4, chunk, LANES), f32),
            pltpu.VMEM((2, 4, chunk, LANES), f32),
            pltpu.VMEM((4, 4, HALO, LANES), f32),
            pltpu.VMEM((span, 3 * side), jnp.bfloat16),
            pltpu.VMEM((3 * side, span), jnp.bfloat16),
            pltpu.VMEM((rows, cols), f32),
            dma((4,)),
            dma((wide_count,)),
            dma((wide_count,)),
            dma,
            dma((wide_count,)),
            dma((wide_count,)),
            dma((2, 8)),
            dma((2, 8)),
            dma((PIECES,)),
        ],
        compiler_params=pltpu.CompilerParams(
            collective_id=0, has_side_effects=True, vmem_limit_bytes=52 * 1024 * 1024
        ),
    )(msg, old_field, stretch_coef, bend_coef, load_field)


def solution(mesh):
    return jax.shard_map(
        local,
        mesh=mesh,
        in_specs=(
            P(("wide", "narrow"), None, None),
            P(("wide", "narrow")),
            P("wide", "narrow"),
            P("wide", "narrow"),
            P("wide", "narrow"),
            P("wide", "narrow"),
        ),
        out_specs=P("wide", "narrow"),
        check_vma=False,
    )
```

```python
import functools

import jax
import jax.numpy as jnp
from jax import lax
from jax.experimental import pallas as pl
from jax.experimental.pallas import tpu as pltpu
from jax.sharding import PartitionSpec as P

SWEEPS = 2
OMEGA = 0.5
CAPACITY = 2
LANES = 128
EDGE = 16
HALO = 8
SLOT = 8
PIECES = 4
MESH = pl.DeviceIdType.MESH


def refine_table(half, rows, cols):
    side = 2 * half
    base = jnp.where(rows >= side, half, 0)
    inner = jnp.where(rows >= side, rows - side, rows)
    near = base + (inner >> 1)
    other = near + jnp.where((inner & 1) == 1, 1, -1)
    other = jnp.minimum(jnp.maximum(other, base), base + half - 1)
    return jnp.where(cols == near, 0.75, 0.0) + jnp.where(cols == other, 0.25, 0.0)


def split3(x):
    high = x.astype(jnp.bfloat16)
    rest = x - high.astype(jnp.float32)
    mid = rest.astype(jnp.bfloat16)
    low = (rest - mid.astype(jnp.float32)).astype(jnp.bfloat16)
    return high, mid, low


def step_of(total):
    return max(k for k in range(8, 65, 8) if total % k == 0)


def laplace(load, count, tiles, ring):
    lane = lax.broadcasted_iota(jnp.int32, (count, LANES), 1)
    kept = {}

    def tile(i):
        if i not in kept:
            kept[i] = {"big": load(i)}
        return kept[i]

    def turned(i, shift):
        held = tile(i)
        if shift not in held:
            held[shift] = pltpu.roll(held["big"][HALO : HALO + count], shift, 1)
        return held[shift]

    for i in tiles:
        big = tile(i)["big"]
        center = big[HALO : HALO + count]
        above = pltpu.roll(big, 1, 0)[HALO : HALO + count]
        below = pltpu.roll(big, count + 2 * HALO - 1, 0)[HALO : HALO + count]
        left = jnp.where(lane == 0, turned((i - 1) % ring, 1), turned(i, 1))
        right = jnp.where(
            lane == LANES - 1, turned((i + 1) % ring, LANES - 1), turned(i, LANES - 1)
        )
        yield i, (above + below) + (left + right) - 4.0 * center, center


def kernel(
    wide_count, narrow_count, groups_x, groups_y,
    source_s, level_s, old_hbm, stretch_hbm, bend_hbm, load_hbm, out_hbm,
    old, table, table_s, send, recv, grid, lap_u, weight, moment, rest, pack, unpacked, corner,
    table_row, table_col, result, msg,
    load_sem, table_send, table_recv, smem_sem, par_send, par_recv, halo_send, halo_recv, out_sem,
):
    me = lax.axis_index("wide")
    seg = lax.axis_index("narrow")
    per_device, side, _ = old.shape
    per_groups = groups_x * groups_y
    span = 2 * side
    rows, cols = groups_x * span, groups_y * span
    width = cols + LANES
    chunk = rows * SLOT // LANES
    has_up, has_down = me > 0, me < wide_count - 1
    has_left, has_right = seg > 0, seg < narrow_count - 1
    up, down = lax.rem(me + wide_count - 1, wide_count), lax.rem(me + 1, wide_count)
    left, right = lax.rem(seg + narrow_count - 1, narrow_count), lax.rem(seg + 1, narrow_count)

    tile_rows = pl.ds(EDGE, rows)
    loads = [
        pltpu.make_async_copy(old_hbm, old, load_sem.at[0]),
        pltpu.make_async_copy(stretch_hbm, grid.at[0, tile_rows, pl.ds(0, cols)], load_sem.at[1]),
        pltpu.make_async_copy(bend_hbm, grid.at[1, tile_rows, pl.ds(0, cols)], load_sem.at[2]),
        pltpu.make_async_copy(load_hbm, grid.at[2, tile_rows, pl.ds(0, cols)], load_sem.at[3]),
    ]
    for copy in loads:
        copy.start()

    at_lane = lax.broadcasted_iota(jnp.int32, msg.shape, 1)
    words = jnp.zeros(msg.shape, jnp.int32)
    for j in range(per_groups):
        words = jnp.where(at_lane == j, source_s[j // groups_y, j % groups_y], words)
    for j in range(per_device):
        words = jnp.where(at_lane == per_groups + j, level_s[j], words)
    msg[...] = words

    peers = [(lax.rem(me + k, wide_count), seg) for k in range(1, wide_count)]
    peers += [(me, left), (me, right), (up, left), (up, right), (down, left), (down, right)]
    barrier = pltpu.get_barrier_semaphore()
    for peer in peers:
        pl.semaphore_signal(barrier, inc=1, device_id=peer, device_id_type=MESH)
    pl.semaphore_wait(barrier, len(peers))

    table_copies = []
    for k in range(1, wide_count):
        copy = pltpu.make_async_remote_copy(
            src_ref=msg, dst_ref=table.at[me], send_sem=table_send.at[k], recv_sem=table_recv.at[k],
            device_id=(lax.rem(me + k, wide_count), seg), device_id_type=MESH,
        )
        copy.start()
        table_copies.append(copy)
    table[me] = msg[...]

    half = side // 2
    shape = (span, side)
    by_row = refine_table(
        half, lax.broadcasted_iota(jnp.int32, shape, 0), lax.broadcasted_iota(jnp.int32, shape, 1)
    ).astype(jnp.bfloat16)
    shape = (side, span)
    by_col = refine_table(
        half, lax.broadcasted_iota(jnp.int32, shape, 1), lax.broadcasted_iota(jnp.int32, shape, 0)
    ).astype(jnp.bfloat16)
    for part in range(3):
        table_row[:, part * side : (part + 1) * side] = by_row
        table_col[part * side : (part + 1) * side, :] = by_col

    for copy in table_copies:
        copy.wait()
    to_smem = pltpu.make_async_copy(table, table_s, smem_sem)
    to_smem.start()
    to_smem.wait()

    loads[0].wait()
    block = per_device * narrow_count

    def picks(dest):
        first, second, seen = jnp.int32(0), jnp.int32(0), jnp.int32(0)
        for j in range(per_groups):
            source = table_s[dest, 0, j]
            mine = lax.div(source, jnp.int32(block)) == me
            where = lax.rem(source, jnp.int32(per_device))
            first = jnp.where(mine & (seen == 0), where, first)
            second = jnp.where(mine & (seen == 1), where, second)
            seen = seen + mine.astype(jnp.int32)
        return first, second

    parent_copies = []
    for k in range(1, wide_count):
        dest = lax.rem(me + k, wide_count)
        first, second = picks(dest)
        send[k, 0] = old[first]
        send[k, 1] = old[second]
        copy = pltpu.make_async_remote_copy(
            src_ref=send.at[k], dst_ref=recv.at[me], send_sem=par_send.at[k], recv_sem=par_recv.at[k],
            device_id=(dest, seg), device_id_type=MESH,
        )
        copy.start()
        parent_copies.append(copy)
    first, second = picks(me)
    recv[me, 0] = old[first]
    recv[me, 1] = old[second]

    ranks = []
    places = []
    for j in range(per_groups):
        source = table_s[me, 0, j]
        rank = lax.div(source, jnp.int32(block))
        slot = jnp.int32(0)
        for earlier in ranks:
            slot = slot + (earlier == rank).astype(jnp.int32)
        ranks.append(rank)
        places.append((rank, jnp.minimum(slot, CAPACITY - 1)))
    loads[1].wait()
    loads[2].wait()
    loads[3].wait()
    for j in range(per_groups):
        source = table_s[me, 0, j]
        level = table_s[ranks[j], 0, per_groups + lax.rem(source, jnp.int32(per_device))]
        factor = jnp.where(level >= 1, 4.0, 1.0).astype(jnp.float32)
        at_row = EDGE + j // groups_y * span
        at_col = j % groups_y * span

        @pl.loop(0, span // 32)
        def _(i):
            here = pl.ds(pl.multiple_of(at_row + i * 32, 8), 32)
            there = pl.ds(at_col, span)
            grid[0, here, there] = grid[0, here, there] * (0.5 * factor)
            grid[1, here, there] = grid[1, here, there] * (factor * factor)

    lane = lax.broadcasted_iota(jnp.int32, (chunk, LANES), 1)

    def exchange(first_plane, planes, phase):
        picked = pl.ds(first_plane, planes)
        for plane in range(first_plane, first_plane + planes):
            to_left = jnp.zeros((chunk, LANES), jnp.float32)
            to_right = to_left
            for i in range(LANES // SLOT):
                here = pl.ds(EDGE + i * chunk, chunk)
                mine = (lane >= i * SLOT) & (lane < (i + 1) * SLOT)
                head = grid[plane, here, 0:LANES]
                tail = grid[plane, here, cols - LANES : cols]
                if i:
                    head = pltpu.roll(head, i * SLOT, 1)
                if (i + 1) * SLOT < LANES:
                    tail = pltpu.roll(tail, (i + 1) * SLOT, 1)
                to_left = jnp.where(mine, head, to_left)
                to_right = jnp.where(mine, tail, to_right)
            pack[0, plane] = to_left
            pack[1, plane] = to_right
        top, bottom = pl.ds(EDGE, HALO), pl.ds(EDGE + rows - HALO, HALO)
        over, under = pl.ds(EDGE - HALO, HALO), pl.ds(EDGE + rows, HALO)
        every = pl.ds(0, cols)
        first, last = pl.ds(0, LANES), pl.ds(cols - LANES, LANES)
        plan = [
            (grid.at[picked, top, every], grid.at[picked, under, every], (up, seg)),
            (grid.at[picked, bottom, every], grid.at[picked, over, every], (down, seg)),
            (pack.at[0, picked], unpacked.at[0, picked], (me, left)),
            (pack.at[1, picked], unpacked.at[1, picked], (me, right)),
            (grid.at[picked, top, first], corner.at[0, picked], (up, left)),
            (grid.at[picked, top, last], corner.at[1, picked], (up, right)),
            (grid.at[picked, bottom, first], corner.at[2, picked], (down, left)),
            (grid.at[picked, bottom, last], corner.at[3, picked], (down, right)),
        ]
        copies = []
        for i, (source, target, device) in enumerate(plan):
            copy = pltpu.make_async_remote_copy(
                src_ref=source, dst_ref=target,
                send_sem=halo_send.at[phase, i], recv_sem=halo_recv.at[phase, i],
                device_id=device, device_id_type=MESH,
            )
            copy.start()
            copies.append(copy)
        return copies

    edge_lane = lax.broadcasted_iota(jnp.int32, (HALO, LANES), 1)

    def settle(copies, first_plane, planes):
        for copy in copies:
            copy.wait()
        beside = pl.ds(cols, LANES)
        for plane in range(first_plane, first_plane + planes):
            from_right, from_left = unpacked[0, plane], unpacked[1, plane]
            inside = jnp.where(lane < LANES // 2, has_right.astype(jnp.int32), has_left.astype(jnp.int32)) > 0
            for i in range(LANES // SLOT):
                head, tail = from_right, from_left
                if i:
                    head = pltpu.roll(head, LANES - i * SLOT, 1)
                if (i + 1) * SLOT < LANES:
                    tail = pltpu.roll(tail, LANES - (i + 1) * SLOT, 1)
                joined = jnp.where(lane < LANES // 2, head, tail)
                grid[plane, pl.ds(EDGE + i * chunk, chunk), beside] = jnp.where(inside, joined, 0.0)
            for at, is_there, pair in ((EDGE + rows, has_down, 0), (EDGE - HALO, has_up, 2)):
                here = pl.ds(at, HALO)
                joined = jnp.where(edge_lane < LANES // 2, corner[pair, plane], corner[pair + 1, plane])
                keep = jnp.where(
                    edge_lane < LANES // 2, has_right.astype(jnp.int32), has_left.astype(jnp.int32)
                ) * is_there.astype(jnp.int32)
                grid[plane, here, beside] = jnp.where(keep > 0, joined, 0.0)
                every = grid[plane, here, 0:cols]
                grid[plane, here, 0:cols] = jnp.where(is_there, every, jnp.zeros_like(every))

    def clear_outside():
        beside = pl.ds(cols, LANES)
        total = rows + 2 * HALO
        inside_lane = lax.broadcasted_iota(jnp.int32, (total, LANES), 1)
        keep = jnp.where(inside_lane < LANES // 2, has_right.astype(jnp.int32), has_left.astype(jnp.int32)) > 0
        here = pl.ds(EDGE - HALO, total)
        grid[3, here, beside] = jnp.where(keep, grid[3, here, beside], 0.0)
        for at, is_there in ((EDGE + rows, has_down), (EDGE - HALO, has_up)):
            here = pl.ds(at, HALO)
            every = grid[3, here, :]
            grid[3, here, :] = jnp.where(is_there, every, jnp.zeros_like(every))

    ring = width // LANES
    whole = list(range(ring))

    def sweep_rows(body, start, total):
        step = step_of(total)

        def one(at):
            around = pl.ds(pl.multiple_of(at - HALO, 8), step + 2 * HALO)
            body(around, pl.ds(pl.multiple_of(at, 8), step), at, step)

        if total == step:
            one(start)
        else:
            pl.loop(0, total // step)(lambda i: one(start + i * step))

    def lanes(i):
        return pl.ds(i * LANES, LANES)

    def coefficients(around, here, at, step):
        of_u = laplace(lambda i: grid[0, around, lanes(i)], step, whole, ring)
        of_b = laplace(lambda i: grid[1, around, lanes(i)], step, whole, ring)
        for (i, lap_a, mid_u), (_, lap_b, mid_b) in zip(of_u, of_b):
            lap_u[here, lanes(i)] = lap_a
            weight[here, lanes(i)] = OMEGA / (lap_a + lap_b + 8.0 * mid_u + 20.0 * mid_b)

    settle(exchange(0, 3, 0), 0, 3)
    sweep_rows(coefficients, EDGE - HALO, rows + 2 * HALO)

    for copy in parent_copies:
        copy.wait()
    for j in range(per_groups):
        rank, slot = places[j]
        parent = recv[rank, slot]
        wider = jnp.dot(
            jnp.concatenate(split3(parent), axis=1), table_col[...], preferred_element_type=jnp.float32
        )
        child = jnp.dot(
            table_row[...], jnp.concatenate(split3(wider), axis=0), preferred_element_type=jnp.float32
        )
        grid[3, pl.ds(EDGE + j // groups_y * span, span), pl.ds(j % groups_y * span, span)] = child

    def first_half(tiles, start, total):
        def body(around, here, at, step):
            for i, of_v, mid in laplace(lambda i: grid[3, around, lanes(i)], step, tiles, ring):
                coef = grid[0, here, lanes(i)]
                moment[here, lanes(i)] = grid[1, here, lanes(i)] * of_v - coef * mid
                rest[here, lanes(i)] = grid[2, here, lanes(i)] - (
                    mid * lap_u[here, lanes(i)] - coef * of_v
                )

        sweep_rows(body, start, total)

    def second_half(tiles, start, total, store):
        def body(around, here, at, step):
            for i, of_m, _ in laplace(lambda i: moment[around, lanes(i)], step, tiles, ring):
                store(
                    at, step, here, i,
                    grid[3, here, lanes(i)] + weight[here, lanes(i)] * (rest[here, lanes(i)] - of_m),
                )

        sweep_rows(body, start, total)

    strip = EDGE + HALO
    copies = exchange(3, 1, 1)
    first_half(whole[1:-2], 2 * EDGE, rows - 2 * EDGE)
    settle(copies, 3, 1)
    first_half(whole[-2:] + whole[:1], 2 * EDGE, rows - 2 * EDGE)
    first_half(whole, EDGE - HALO, strip)
    first_half(whole, rows, strip)

    def keep_field(at, step, here, i, value):
        grid[3, here, lanes(i)] = value

    def keep_result(at, step, here, i, value):
        result[pl.ds(pl.multiple_of(at - EDGE, 8), step), lanes(i)] = value

    for sweep in range(SWEEPS):
        if sweep:
            first_half(whole, EDGE - HALO, rows + 2 * HALO)
        if sweep < SWEEPS - 1:
            second_half(whole, EDGE - HALO, rows + 2 * HALO, keep_field)
            clear_outside()
    piece = rows // PIECES
    stores = []
    for p in range(PIECES):
        second_half(whole[:-1], EDGE + p * piece, piece, keep_result)
        part = pl.ds(p * piece, piece)
        copy = pltpu.make_async_copy(result.at[part, :], out_hbm.at[part, :], out_sem.at[p])
        copy.start()
        stores.append(copy)
    for copy in stores:
        copy.wait()


def local(old_field, old_level, new_source, stretch_coef, bend_coef, load_field):
    wide_count = lax.axis_size("wide")
    narrow_count = lax.axis_size("narrow")
    groups_x, groups_y = new_source.shape
    per_device, side, _ = old_field.shape
    rows, cols = stretch_coef.shape
    used = groups_x * groups_y + per_device
    length = -(-used // LANES) * LANES
    full = (rows + 2 * EDGE, cols + LANES)
    chunk = rows * SLOT // LANES
    span = 2 * side
    f32 = jnp.float32
    dma = pltpu.SemaphoreType.DMA
    return pl.pallas_call(
        functools.partial(kernel, wide_count, narrow_count, groups_x, groups_y),
        out_shape=jax.ShapeDtypeStruct((rows, cols), f32),
        in_specs=[pl.BlockSpec(memory_space=pltpu.SMEM)] * 2 + [pl.BlockSpec(memory_space=pl.ANY)] * 4,
        out_specs=pl.BlockSpec(memory_space=pl.ANY),
        scratch_shapes=[
            pltpu.VMEM(old_field.shape, f32),
            pltpu.VMEM((wide_count, 1, length), jnp.int32),
            pltpu.SMEM((wide_count, 1, length), jnp.int32),
            pltpu.VMEM((wide_count, CAPACITY, side, side), f32),
            pltpu.VMEM((wide_count, CAPACITY, side, side), f32),
            pltpu.VMEM((4,) + full, f32),
            pltpu.VMEM(full, f32),
            pltpu.VMEM(full, f32),
            pltpu.VMEM(full, f32),
            pltpu.VMEM(full, f32),
            pltpu.VMEM((2, 4, chunk, LANES), f32),
            pltpu.VMEM((2, 4, chunk, LANES), f32),
            pltpu.VMEM((4, 4, HALO, LANES), f32),
            pltpu.VMEM((span, 3 * side), jnp.bfloat16),
            pltpu.VMEM((3 * side, span), jnp.bfloat16),
            pltpu.VMEM((rows, cols), f32),
            pltpu.VMEM((1, length), jnp.int32),
            dma((4,)),
            dma((wide_count,)),
            dma((wide_count,)),
            dma,
            dma((wide_count,)),
            dma((wide_count,)),
            dma((2, 8)),
            dma((2, 8)),
            dma((PIECES,)),
        ],
        compiler_params=pltpu.CompilerParams(
            collective_id=0, has_side_effects=True, vmem_limit_bytes=52 * 1024 * 1024
        ),
    )(new_source, old_level, old_field, stretch_coef, bend_coef, load_field)


def solution(mesh):
    return jax.shard_map(
        local,
        mesh=mesh,
        in_specs=(
            P(("wide", "narrow"), None, None),
            P(("wide", "narrow")),
            P("wide", "narrow"),
            P("wide", "narrow"),
            P("wide", "narrow"),
            P("wide", "narrow"),
        ),
        out_specs=P("wide", "narrow"),
        check_vma=False,
    )
```

```python
import functools

import jax
import jax.numpy as jnp
from jax import lax
from jax.experimental import pallas as pl
from jax.experimental.pallas import tpu as pltpu
from jax.sharding import PartitionSpec as P

SWEEPS = 2
OMEGA = 0.5
CAPACITY = 2
LANES = 128
EDGE = 16
HALO = 8
SLOT = 8
PIECES = 4
MESH = pl.DeviceIdType.MESH


def refine_table(half, rows, cols):
    side = 2 * half
    base = jnp.where(rows >= side, half, 0)
    inner = jnp.where(rows >= side, rows - side, rows)
    near = base + (inner >> 1)
    other = near + jnp.where((inner & 1) == 1, 1, -1)
    other = jnp.minimum(jnp.maximum(other, base), base + half - 1)
    return jnp.where(cols == near, 0.75, 0.0) + jnp.where(cols == other, 0.25, 0.0)


def split3(x):
    high = x.astype(jnp.bfloat16)
    rest = x - high.astype(jnp.float32)
    mid = rest.astype(jnp.bfloat16)
    low = (rest - mid.astype(jnp.float32)).astype(jnp.bfloat16)
    return high, mid, low


def step_of(total):
    return max(k for k in range(8, 65, 8) if total % k == 0)


def laplace(load, count, tiles, ring):
    lane = lax.broadcasted_iota(jnp.int32, (count, LANES), 1)
    kept = {}

    def tile(i):
        if i not in kept:
            kept[i] = {"center": load(i, 0)}
        return kept[i]

    def turned(i, shift):
        held = tile(i)
        if shift not in held:
            held[shift] = pltpu.roll(held["center"], shift, 1)
        return held[shift]

    for i in tiles:
        center, above, below = tile(i)["center"], load(i, -1), load(i, 1)
        left = jnp.where(lane == 0, turned((i - 1) % ring, 1), turned(i, 1))
        right = jnp.where(
            lane == LANES - 1, turned((i + 1) % ring, LANES - 1), turned(i, LANES - 1)
        )
        yield i, (above + below) + (left + right) - 4.0 * center, center


def kernel(
    wide_count, narrow_count, groups_x, groups_y,
    source_s, level_s, old_hbm, stretch_hbm, bend_hbm, load_hbm, out_hbm,
    old, table, table_s, send, recv, grid, lap_u, weight, moment, rest, pack, unpacked, corner,
    table_row, table_col, result, msg,
    load_sem, table_send, table_recv, smem_sem, par_send, par_recv, halo_send, halo_recv, out_sem,
):
    me = lax.axis_index("wide")
    seg = lax.axis_index("narrow")
    per_device, side, _ = old.shape
    per_groups = groups_x * groups_y
    span = 2 * side
    rows, cols = groups_x * span, groups_y * span
    chunk = rows * SLOT // LANES
    has_up, has_down = me > 0, me < wide_count - 1
    has_left, has_right = seg > 0, seg < narrow_count - 1
    up, down = lax.rem(me + wide_count - 1, wide_count), lax.rem(me + 1, wide_count)
    left, right = lax.rem(seg + narrow_count - 1, narrow_count), lax.rem(seg + 1, narrow_count)

    tile_rows = pl.ds(EDGE, rows)
    tiles = cols // LANES
    ring = tiles + 1
    loads = [pltpu.make_async_copy(old_hbm, old, load_sem.at[0])]
    for plane, source in enumerate((stretch_hbm, bend_hbm, load_hbm)):
        for i in range(tiles):
            loads.append(
                pltpu.make_async_copy(
                    source.at[:, pl.ds(i * LANES, LANES)],
                    grid.at[plane, i, tile_rows, :],
                    load_sem.at[1 + plane * tiles + i],
                )
            )
    for copy in loads:
        copy.start()

    at_lane = lax.broadcasted_iota(jnp.int32, msg.shape, 1)
    words = jnp.zeros(msg.shape, jnp.int32)
    for j in range(per_groups):
        words = jnp.where(at_lane == j, source_s[j // groups_y, j % groups_y], words)
    for j in range(per_device):
        words = jnp.where(at_lane == per_groups + j, level_s[j], words)
    msg[...] = words

    peers = [(lax.rem(me + k, wide_count), seg) for k in range(1, wide_count)]
    peers += [(me, left), (me, right), (up, left), (up, right), (down, left), (down, right)]
    barrier = pltpu.get_barrier_semaphore()
    for peer in peers:
        pl.semaphore_signal(barrier, inc=1, device_id=peer, device_id_type=MESH)
    pl.semaphore_wait(barrier, len(peers))

    table_copies = []
    for k in range(1, wide_count):
        copy = pltpu.make_async_remote_copy(
            src_ref=msg, dst_ref=table.at[me], send_sem=table_send.at[k], recv_sem=table_recv.at[k],
            device_id=(lax.rem(me + k, wide_count), seg), device_id_type=MESH,
        )
        copy.start()
        table_copies.append(copy)
    table[me] = msg[...]

    half = side // 2
    shape = (span, side)
    by_row = refine_table(
        half, lax.broadcasted_iota(jnp.int32, shape, 0), lax.broadcasted_iota(jnp.int32, shape, 1)
    ).astype(jnp.bfloat16)
    shape = (side, span)
    by_col = refine_table(
        half, lax.broadcasted_iota(jnp.int32, shape, 1), lax.broadcasted_iota(jnp.int32, shape, 0)
    ).astype(jnp.bfloat16)
    for part in range(3):
        table_row[:, part * side : (part + 1) * side] = by_row
        table_col[part * side : (part + 1) * side, :] = by_col

    for copy in table_copies:
        copy.wait()
    to_smem = pltpu.make_async_copy(table, table_s, smem_sem)
    to_smem.start()
    to_smem.wait()

    loads[0].wait()
    block = per_device * narrow_count

    def picks(dest):
        first, second, seen = jnp.int32(0), jnp.int32(0), jnp.int32(0)
        for j in range(per_groups):
            source = table_s[dest, 0, j]
            mine = lax.div(source, jnp.int32(block)) == me
            where = lax.rem(source, jnp.int32(per_device))
            first = jnp.where(mine & (seen == 0), where, first)
            second = jnp.where(mine & (seen == 1), where, second)
            seen = seen + mine.astype(jnp.int32)
        return first, second

    parent_copies = []
    for k in range(1, wide_count):
        dest = lax.rem(me + k, wide_count)
        first, second = picks(dest)
        send[k, 0] = old[first]
        send[k, 1] = old[second]
        copy = pltpu.make_async_remote_copy(
            src_ref=send.at[k], dst_ref=recv.at[me], send_sem=par_send.at[k], recv_sem=par_recv.at[k],
            device_id=(dest, seg), device_id_type=MESH,
        )
        copy.start()
        parent_copies.append(copy)
    first, second = picks(me)
    recv[me, 0] = old[first]
    recv[me, 1] = old[second]

    ranks = []
    places = []
    for j in range(per_groups):
        source = table_s[me, 0, j]
        rank = lax.div(source, jnp.int32(block))
        slot = jnp.int32(0)
        for earlier in ranks:
            slot = slot + (earlier == rank).astype(jnp.int32)
        ranks.append(rank)
        places.append((rank, jnp.minimum(slot, CAPACITY - 1)))
    for copy in loads[1:]:
        copy.wait()
    for j in range(per_groups):
        source = table_s[me, 0, j]
        level = table_s[ranks[j], 0, per_groups + lax.rem(source, jnp.int32(per_device))]
        factor = jnp.where(level >= 1, 4.0, 1.0).astype(jnp.float32)
        at_row = EDGE + j // groups_y * span
        at_col = j % groups_y * span

        @pl.loop(0, span // 32)
        def _(i):
            here = pl.ds(pl.multiple_of(at_row + i * 32, 8), 32)
            for t in range(at_col // LANES, (at_col + span) // LANES):
                grid[0, t, here, :] = grid[0, t, here, :] * (0.5 * factor)
                grid[1, t, here, :] = grid[1, t, here, :] * (factor * factor)

    lane = lax.broadcasted_iota(jnp.int32, (chunk, LANES), 1)

    def exchange(first_plane, planes, phase):
        picked = pl.ds(first_plane, planes)
        for plane in range(first_plane, first_plane + planes):
            to_left = jnp.zeros((chunk, LANES), jnp.float32)
            to_right = to_left
            for i in range(LANES // SLOT):
                here = pl.ds(EDGE + i * chunk, chunk)
                mine = (lane >= i * SLOT) & (lane < (i + 1) * SLOT)
                head = grid[plane, 0, here, :]
                tail = grid[plane, tiles - 1, here, :]
                if i:
                    head = pltpu.roll(head, i * SLOT, 1)
                if (i + 1) * SLOT < LANES:
                    tail = pltpu.roll(tail, (i + 1) * SLOT, 1)
                to_left = jnp.where(mine, head, to_left)
                to_right = jnp.where(mine, tail, to_right)
            pack[0, plane] = to_left
            pack[1, plane] = to_right
        top, bottom = pl.ds(EDGE, HALO), pl.ds(EDGE + rows - HALO, HALO)
        over, under = pl.ds(EDGE - HALO, HALO), pl.ds(EDGE + rows, HALO)
        every = pl.ds(0, tiles)
        first, last = 0, tiles - 1
        plan = [
            (grid.at[picked, every, top, :], grid.at[picked, every, under, :], (up, seg)),
            (grid.at[picked, every, bottom, :], grid.at[picked, every, over, :], (down, seg)),
            (pack.at[0, picked], unpacked.at[0, picked], (me, left)),
            (pack.at[1, picked], unpacked.at[1, picked], (me, right)),
            (grid.at[picked, first, top, :], corner.at[0, picked], (up, left)),
            (grid.at[picked, last, top, :], corner.at[1, picked], (up, right)),
            (grid.at[picked, first, bottom, :], corner.at[2, picked], (down, left)),
            (grid.at[picked, last, bottom, :], corner.at[3, picked], (down, right)),
        ]
        copies = []
        for i, (source, target, device) in enumerate(plan):
            copy = pltpu.make_async_remote_copy(
                src_ref=source, dst_ref=target,
                send_sem=halo_send.at[phase, i], recv_sem=halo_recv.at[phase, i],
                device_id=device, device_id_type=MESH,
            )
            copy.start()
            copies.append(copy)
        return copies

    edge_lane = lax.broadcasted_iota(jnp.int32, (HALO, LANES), 1)

    def settle(copies, first_plane, planes):
        for copy in copies:
            copy.wait()
        beside = tiles
        for plane in range(first_plane, first_plane + planes):
            from_right, from_left = unpacked[0, plane], unpacked[1, plane]
            inside = jnp.where(lane < LANES // 2, has_right.astype(jnp.int32), has_left.astype(jnp.int32)) > 0
            for i in range(LANES // SLOT):
                head, tail = from_right, from_left
                if i:
                    head = pltpu.roll(head, LANES - i * SLOT, 1)
                if (i + 1) * SLOT < LANES:
                    tail = pltpu.roll(tail, LANES - (i + 1) * SLOT, 1)
                joined = jnp.where(lane < LANES // 2, head, tail)
                grid[plane, beside, pl.ds(EDGE + i * chunk, chunk), :] = jnp.where(inside, joined, 0.0)
            for at, is_there, pair in ((EDGE + rows, has_down, 0), (EDGE - HALO, has_up, 2)):
                here = pl.ds(at, HALO)
                joined = jnp.where(edge_lane < LANES // 2, corner[pair, plane], corner[pair + 1, plane])
                keep = jnp.where(
                    edge_lane < LANES // 2, has_right.astype(jnp.int32), has_left.astype(jnp.int32)
                ) * is_there.astype(jnp.int32)
                grid[plane, beside, here, :] = jnp.where(keep > 0, joined, 0.0)
                every = grid[plane, 0:tiles, here, :]
                grid[plane, 0:tiles, here, :] = jnp.where(is_there, every, jnp.zeros_like(every))

    def clear_outside():
        beside = tiles
        total = rows + 2 * HALO
        inside_lane = lax.broadcasted_iota(jnp.int32, (total, LANES), 1)
        keep = jnp.where(inside_lane < LANES // 2, has_right.astype(jnp.int32), has_left.astype(jnp.int32)) > 0
        here = pl.ds(EDGE - HALO, total)
        grid[3, beside, here, :] = jnp.where(keep, grid[3, beside, here, :], 0.0)
        for at, is_there in ((EDGE + rows, has_down), (EDGE - HALO, has_up)):
            here = pl.ds(at, HALO)
            every = grid[3, :, here, :]
            grid[3, :, here, :] = jnp.where(is_there, every, jnp.zeros_like(every))

    whole = list(range(ring))

    def sweep_rows(body, start, total):
        step = step_of(total)

        def one(at):
            body(pl.ds(pl.multiple_of(at, 8), step), at, step)

        if total == step:
            one(start)
        else:
            pl.loop(0, total // step)(lambda i: one(start + i * step))

    def near(ref, at, step):
        return lambda i, shift: ref[i, pl.ds(pl.multiple_of(at, 8) + shift, step), :]

    def coefficients(here, at, step):
        of_u = laplace(near(grid.at[0], at, step), step, whole, ring)
        of_b = laplace(near(grid.at[1], at, step), step, whole, ring)
        for (i, lap_a, mid_u), (_, lap_b, mid_b) in zip(of_u, of_b):
            lap_u[i, here, :] = lap_a
            weight[i, here, :] = OMEGA / (lap_a + lap_b + 8.0 * mid_u + 20.0 * mid_b)

    settle(exchange(0, 3, 0), 0, 3)
    sweep_rows(coefficients, EDGE - HALO, rows + 2 * HALO)

    for copy in parent_copies:
        copy.wait()
    for j in range(per_groups):
        rank, slot = places[j]
        parent = recv[rank, slot]
        wider = jnp.dot(
            jnp.concatenate(split3(parent), axis=1), table_col[...], preferred_element_type=jnp.float32
        )
        child = jnp.dot(
            table_row[...], jnp.concatenate(split3(wider), axis=0), preferred_element_type=jnp.float32
        )
        for t in range(span // LANES):
            here = pl.ds(EDGE + j // groups_y * span, span)
            grid[3, j % groups_y * (span // LANES) + t, here, :] = child[:, t * LANES : (t + 1) * LANES]

    def first_half(tiles, start, total):
        def body(here, at, step):
            for i, of_v, mid in laplace(near(grid.at[3], at, step), step, tiles, ring):
                coef = grid[0, i, here, :]
                moment[i, here, :] = grid[1, i, here, :] * of_v - coef * mid
                rest[i, here, :] = grid[2, i, here, :] - (
                    mid * lap_u[i, here, :] - coef * of_v
                )

        sweep_rows(body, start, total)

    def second_half(tiles, start, total, store):
        def body(here, at, step):
            for i, of_m, _ in laplace(near(moment, at, step), step, tiles, ring):
                store(
                    at, step, here, i,
                    grid[3, i, here, :] + weight[i, here, :] * (rest[i, here, :] - of_m),
                )

        sweep_rows(body, start, total)

    strip = EDGE + HALO
    copies = exchange(3, 1, 1)
    first_half(whole[1:-2], 2 * EDGE, rows - 2 * EDGE)
    settle(copies, 3, 1)
    first_half(whole[-2:] + whole[:1], 2 * EDGE, rows - 2 * EDGE)
    first_half(whole, EDGE - HALO, strip)
    first_half(whole, rows, strip)

    def keep_field(at, step, here, i, value):
        grid[3, i, here, :] = value

    def keep_result(at, step, here, i, value):
        result[i, pl.ds(pl.multiple_of(at - EDGE, 8), step), :] = value

    for sweep in range(SWEEPS):
        if sweep:
            first_half(whole, EDGE - HALO, rows + 2 * HALO)
        if sweep < SWEEPS - 1:
            second_half(whole, EDGE - HALO, rows + 2 * HALO, keep_field)
            clear_outside()
    piece = rows // PIECES
    stores = []
    for p in range(PIECES):
        second_half(whole[:-1], EDGE + p * piece, piece, keep_result)
        part = pl.ds(p * piece, piece)
        for i in range(tiles):
            copy = pltpu.make_async_copy(
                result.at[i, part, :],
                out_hbm.at[part, pl.ds(i * LANES, LANES)],
                out_sem.at[p * tiles + i],
            )
            copy.start()
            stores.append(copy)
    for copy in stores:
        copy.wait()


def local(old_field, old_level, new_source, stretch_coef, bend_coef, load_field):
    wide_count = lax.axis_size("wide")
    narrow_count = lax.axis_size("narrow")
    groups_x, groups_y = new_source.shape
    per_device, side, _ = old_field.shape
    rows, cols = stretch_coef.shape
    used = groups_x * groups_y + per_device
    length = -(-used // LANES) * LANES
    tiles = cols // LANES
    full = (tiles + 1, rows + 2 * EDGE, LANES)
    chunk = rows * SLOT // LANES
    span = 2 * side
    f32 = jnp.float32
    dma = pltpu.SemaphoreType.DMA
    return pl.pallas_call(
        functools.partial(kernel, wide_count, narrow_count, groups_x, groups_y),
        out_shape=jax.ShapeDtypeStruct((rows, cols), f32),
        in_specs=[pl.BlockSpec(memory_space=pltpu.SMEM)] * 2 + [pl.BlockSpec(memory_space=pl.ANY)] * 4,
        out_specs=pl.BlockSpec(memory_space=pl.ANY),
        scratch_shapes=[
            pltpu.VMEM(old_field.shape, f32),
            pltpu.VMEM((wide_count, 1, length), jnp.int32),
            pltpu.SMEM((wide_count, 1, length), jnp.int32),
            pltpu.VMEM((wide_count, CAPACITY, side, side), f32),
            pltpu.VMEM((wide_count, CAPACITY, side, side), f32),
            pltpu.VMEM((4,) + full, f32),
            pltpu.VMEM(full, f32),
            pltpu.VMEM(full, f32),
            pltpu.VMEM(full, f32),
            pltpu.VMEM(full, f32),
            pltpu.VMEM((2, 4, chunk, LANES), f32),
            pltpu.VMEM((2, 4, chunk, LANES), f32),
            pltpu.VMEM((4, 4, HALO, LANES), f32),
            pltpu.VMEM((span, 3 * side), jnp.bfloat16),
            pltpu.VMEM((3 * side, span), jnp.bfloat16),
            pltpu.VMEM((tiles, rows, LANES), f32),
            pltpu.VMEM((1, length), jnp.int32),
            dma((1 + 3 * tiles,)),
            dma((wide_count,)),
            dma((wide_count,)),
            dma,
            dma((wide_count,)),
            dma((wide_count,)),
            dma((2, 8)),
            dma((2, 8)),
            dma((PIECES * tiles,)),
        ],
        compiler_params=pltpu.CompilerParams(
            collective_id=0, has_side_effects=True, vmem_limit_bytes=52 * 1024 * 1024
        ),
    )(new_source, old_level, old_field, stretch_coef, bend_coef, load_field)


def solution(mesh):
    return jax.shard_map(
        local,
        mesh=mesh,
        in_specs=(
            P(("wide", "narrow"), None, None),
            P(("wide", "narrow")),
            P("wide", "narrow"),
            P("wide", "narrow"),
            P("wide", "narrow"),
            P("wide", "narrow"),
        ),
        out_specs=P("wide", "narrow"),
        check_vma=False,
    )
```

```python
import functools

import jax
import jax.numpy as jnp
from jax import lax
from jax.experimental import pallas as pl
from jax.experimental.pallas import tpu as pltpu
from jax.sharding import PartitionSpec as P

SWEEPS = 2
OMEGA = 0.5
CAPACITY = 2
LANES = 128
EDGE = 16
HALO = 8
SLOT = 8
PIECES = 4
MESH = pl.DeviceIdType.MESH


def refine_table(half, rows, cols):
    side = 2 * half
    base = jnp.where(rows >= side, half, 0)
    inner = jnp.where(rows >= side, rows - side, rows)
    near = base + (inner >> 1)
    other = near + jnp.where((inner & 1) == 1, 1, -1)
    other = jnp.minimum(jnp.maximum(other, base), base + half - 1)
    return jnp.where(cols == near, 0.75, 0.0) + jnp.where(cols == other, 0.25, 0.0)


def split3(x):
    high = x.astype(jnp.bfloat16)
    rest = x - high.astype(jnp.float32)
    mid = rest.astype(jnp.bfloat16)
    low = (rest - mid.astype(jnp.float32)).astype(jnp.bfloat16)
    return high, mid, low


def step_of(total):
    return max(k for k in range(8, 65, 8) if total % k == 0)


def laplace(load, count, tiles, ring):
    lane = lax.broadcasted_iota(jnp.int32, (count, LANES), 1)
    kept = {}

    def tile(i):
        if i not in kept:
            kept[i] = {"center": load(i, 0)}
        return kept[i]

    def turned(i, shift):
        held = tile(i)
        if shift not in held:
            held[shift] = pltpu.roll(held["center"], shift, 1)
        return held[shift]

    for i in tiles:
        center, above, below = tile(i)["center"], load(i, -1), load(i, 1)
        left = jnp.where(lane == 0, turned((i - 1) % ring, 1), turned(i, 1))
        right = jnp.where(
            lane == LANES - 1, turned((i + 1) % ring, LANES - 1), turned(i, LANES - 1)
        )
        yield i, (above + below) + (left + right) - 4.0 * center, center


def kernel(
    wide_count, narrow_count, groups_x, groups_y,
    source_s, level_s, old_hbm, stretch_hbm, bend_hbm, load_hbm, out_hbm,
    old, table, table_s, send, recv, grid, lap_u, weight, moment, rest, pack, unpacked, corner,
    table_row, table_col, result, msg,
    load_sem, table_send, table_recv, smem_sem, par_send, par_recv, halo_send, halo_recv, out_sem,
):
    me = lax.axis_index("wide")
    seg = lax.axis_index("narrow")
    per_device, side, _ = old.shape
    per_groups = groups_x * groups_y
    span = 2 * side
    rows, cols = groups_x * span, groups_y * span
    chunk = rows * SLOT // LANES
    has_up, has_down = me > 0, me < wide_count - 1
    has_left, has_right = seg > 0, seg < narrow_count - 1
    up, down = lax.rem(me + wide_count - 1, wide_count), lax.rem(me + 1, wide_count)
    left, right = lax.rem(seg + narrow_count - 1, narrow_count), lax.rem(seg + 1, narrow_count)

    tile_rows = pl.ds(EDGE, rows)
    tiles = cols // LANES
    ring = tiles + 1
    loads = [pltpu.make_async_copy(old_hbm, old, load_sem.at[0])]
    for plane, source in enumerate((stretch_hbm, bend_hbm, load_hbm)):
        for i in range(tiles):
            loads.append(
                pltpu.make_async_copy(
                    source.at[:, pl.ds(i * LANES, LANES)],
                    grid.at[plane, i, tile_rows, :],
                    load_sem.at[1 + plane * tiles + i],
                )
            )
    for copy in loads:
        copy.start()

    at_lane = lax.broadcasted_iota(jnp.int32, msg.shape, 1)
    words = jnp.zeros(msg.shape, jnp.int32)
    for j in range(per_groups):
        words = jnp.where(at_lane == j, source_s[j // groups_y, j % groups_y], words)
    for j in range(per_device):
        words = jnp.where(at_lane == per_groups + j, level_s[j], words)
    msg[...] = words

    peers = [(lax.rem(me + k, wide_count), seg) for k in range(1, wide_count)]
    peers += [(me, left), (me, right), (up, left), (up, right), (down, left), (down, right)]
    barrier = pltpu.get_barrier_semaphore()
    for peer in peers:
        pl.semaphore_signal(barrier, inc=1, device_id=peer, device_id_type=MESH)
    pl.semaphore_wait(barrier, len(peers))

    table_copies = []
    for k in range(1, wide_count):
        copy = pltpu.make_async_remote_copy(
            src_ref=msg, dst_ref=table.at[me], send_sem=table_send.at[k], recv_sem=table_recv.at[k],
            device_id=(lax.rem(me + k, wide_count), seg), device_id_type=MESH,
        )
        copy.start()
        table_copies.append(copy)
    table[me] = msg[...]

    half = side // 2
    shape = (span, side)
    by_row = refine_table(
        half, lax.broadcasted_iota(jnp.int32, shape, 0), lax.broadcasted_iota(jnp.int32, shape, 1)
    ).astype(jnp.bfloat16)
    shape = (side, span)
    by_col = refine_table(
        half, lax.broadcasted_iota(jnp.int32, shape, 1), lax.broadcasted_iota(jnp.int32, shape, 0)
    ).astype(jnp.bfloat16)
    for part in range(3):
        table_row[:, part * side : (part + 1) * side] = by_row
        table_col[part * side : (part + 1) * side, :] = by_col

    for copy in table_copies:
        copy.wait()
    to_smem = pltpu.make_async_copy(table, table_s, smem_sem)
    to_smem.start()
    to_smem.wait()

    loads[0].wait()
    block = per_device * narrow_count

    def picks(dest):
        first, second, seen = jnp.int32(0), jnp.int32(0), jnp.int32(0)
        for j in range(per_groups):
            source = table_s[dest, 0, j]
            mine = lax.div(source, jnp.int32(block)) == me
            where = lax.rem(source, jnp.int32(per_device))
            first = jnp.where(mine & (seen == 0), where, first)
            second = jnp.where(mine & (seen == 1), where, second)
            seen = seen + mine.astype(jnp.int32)
        return first, second

    parent_copies = []
    for k in range(1, wide_count):
        dest = lax.rem(me + k, wide_count)
        first, second = picks(dest)
        send[k, 0] = old[first]
        send[k, 1] = old[second]
        copy = pltpu.make_async_remote_copy(
            src_ref=send.at[k], dst_ref=recv.at[me], send_sem=par_send.at[k], recv_sem=par_recv.at[k],
            device_id=(dest, seg), device_id_type=MESH,
        )
        copy.start()
        parent_copies.append(copy)
    first, second = picks(me)
    recv[me, 0] = old[first]
    recv[me, 1] = old[second]

    ranks = []
    places = []
    for j in range(per_groups):
        source = table_s[me, 0, j]
        rank = lax.div(source, jnp.int32(block))
        slot = jnp.int32(0)
        for earlier in ranks:
            slot = slot + (earlier == rank).astype(jnp.int32)
        ranks.append(rank)
        places.append((rank, jnp.minimum(slot, CAPACITY - 1)))
    for copy in loads[1:]:
        copy.wait()
    for j in range(per_groups):
        source = table_s[me, 0, j]
        level = table_s[ranks[j], 0, per_groups + lax.rem(source, jnp.int32(per_device))]
        factor = jnp.where(level >= 1, 4.0, 1.0).astype(jnp.float32)
        at_row = EDGE + j // groups_y * span
        at_col = j % groups_y * span

        @pl.loop(0, span // 32)
        def _(i):
            here = pl.ds(pl.multiple_of(at_row + i * 32, 8), 32)
            for t in range(at_col // LANES, (at_col + span) // LANES):
                grid[0, t, here, :] = grid[0, t, here, :] * (0.5 * factor)
                grid[1, t, here, :] = grid[1, t, here, :] * (factor * factor)

    lane = lax.broadcasted_iota(jnp.int32, (chunk, LANES), 1)

    def exchange(first_plane, planes, phase):
        picked = pl.ds(first_plane, planes)
        for plane in range(first_plane, first_plane + planes):
            to_left = jnp.zeros((chunk, LANES), jnp.float32)
            to_right = to_left
            for i in range(LANES // SLOT):
                here = pl.ds(EDGE + i * chunk, chunk)
                mine = (lane >= i * SLOT) & (lane < (i + 1) * SLOT)
                head = grid[plane, 0, here, :]
                tail = grid[plane, tiles - 1, here, :]
                if i:
                    head = pltpu.roll(head, i * SLOT, 1)
                if (i + 1) * SLOT < LANES:
                    tail = pltpu.roll(tail, (i + 1) * SLOT, 1)
                to_left = jnp.where(mine, head, to_left)
                to_right = jnp.where(mine, tail, to_right)
            pack[0, plane] = to_left
            pack[1, plane] = to_right
        top, bottom = pl.ds(EDGE, HALO), pl.ds(EDGE + rows - HALO, HALO)
        over, under = pl.ds(EDGE - HALO, HALO), pl.ds(EDGE + rows, HALO)
        every = pl.ds(0, tiles)
        first, last = 0, tiles - 1
        plan = [
            (grid.at[picked, every, top, :], grid.at[picked, every, under, :], (up, seg)),
            (grid.at[picked, every, bottom, :], grid.at[picked, every, over, :], (down, seg)),
            (pack.at[0, picked], unpacked.at[0, picked], (me, left)),
            (pack.at[1, picked], unpacked.at[1, picked], (me, right)),
            (grid.at[picked, first, top, :], corner.at[0, picked], (up, left)),
            (grid.at[picked, last, top, :], corner.at[1, picked], (up, right)),
            (grid.at[picked, first, bottom, :], corner.at[2, picked], (down, left)),
            (grid.at[picked, last, bottom, :], corner.at[3, picked], (down, right)),
        ]
        copies = []
        for i, (source, target, device) in enumerate(plan):
            copy = pltpu.make_async_remote_copy(
                src_ref=source, dst_ref=target,
                send_sem=halo_send.at[phase, i], recv_sem=halo_recv.at[phase, i],
                device_id=device, device_id_type=MESH,
            )
            copy.start()
            copies.append(copy)
        return copies

    edge_lane = lax.broadcasted_iota(jnp.int32, (HALO, LANES), 1)

    def settle(copies, first_plane, planes):
        for copy in copies:
            copy.wait()
        beside = tiles
        for plane in range(first_plane, first_plane + planes):
            from_right, from_left = unpacked[0, plane], unpacked[1, plane]
            inside = jnp.where(lane < LANES // 2, has_right.astype(jnp.int32), has_left.astype(jnp.int32)) > 0
            for i in range(LANES // SLOT):
                head, tail = from_right, from_left
                if i:
                    head = pltpu.roll(head, LANES - i * SLOT, 1)
                if (i + 1) * SLOT < LANES:
                    tail = pltpu.roll(tail, LANES - (i + 1) * SLOT, 1)
                joined = jnp.where(lane < LANES // 2, head, tail)
                grid[plane, beside, pl.ds(EDGE + i * chunk, chunk), :] = jnp.where(inside, joined, 0.0)
            for at, is_there, pair in ((EDGE + rows, has_down, 0), (EDGE - HALO, has_up, 2)):
                here = pl.ds(at, HALO)
                joined = jnp.where(edge_lane < LANES // 2, corner[pair, plane], corner[pair + 1, plane])
                keep = jnp.where(
                    edge_lane < LANES // 2, has_right.astype(jnp.int32), has_left.astype(jnp.int32)
                ) * is_there.astype(jnp.int32)
                grid[plane, beside, here, :] = jnp.where(keep > 0, joined, 0.0)
                every = grid[plane, 0:tiles, here, :]
                grid[plane, 0:tiles, here, :] = jnp.where(is_there, every, jnp.zeros_like(every))

    def clear_outside():
        beside = tiles
        total = rows + 2 * HALO
        inside_lane = lax.broadcasted_iota(jnp.int32, (total, LANES), 1)
        keep = jnp.where(inside_lane < LANES // 2, has_right.astype(jnp.int32), has_left.astype(jnp.int32)) > 0
        here = pl.ds(EDGE - HALO, total)
        grid[3, beside, here, :] = jnp.where(keep, grid[3, beside, here, :], 0.0)
        for at, is_there in ((EDGE + rows, has_down), (EDGE - HALO, has_up)):
            here = pl.ds(at, HALO)
            every = grid[3, :, here, :]
            grid[3, :, here, :] = jnp.where(is_there, every, jnp.zeros_like(every))

    whole = list(range(ring))

    def sweep_rows(body, start, total):
        step = step_of(total)

        def one(at):
            body(pl.ds(pl.multiple_of(at, 8), step), at, step)

        if total == step:
            one(start)
        else:
            pl.loop(0, total // step)(lambda i: one(start + i * step))

    def near(ref, at, step):
        return lambda i, shift: ref[i, pl.ds(pl.multiple_of(at, 8) + shift, step), :]

    def coefficients(picked, start, total):
        def body(here, at, step):
            of_u = laplace(near(grid.at[0], at, step), step, picked, ring)
            of_b = laplace(near(grid.at[1], at, step), step, picked, ring)
            for (i, lap_a, mid_u), (_, lap_b, mid_b) in zip(of_u, of_b):
                lap_u[i, here, :] = lap_a
                weight[i, here, :] = OMEGA / (lap_a + lap_b + 8.0 * mid_u + 20.0 * mid_b)

        sweep_rows(body, start, total)

    def inside(half):
        half(whole[1:-2], 2 * EDGE, rows - 2 * EDGE)

    def beside(half):
        half(whole[-2:] + whole[:1], 2 * EDGE, rows - 2 * EDGE)
        half(whole, EDGE - HALO, EDGE + HALO)
        half(whole, rows, EDGE + HALO)

    coef_copies = exchange(0, 3, 0)
    inside(coefficients)

    for copy in parent_copies:
        copy.wait()
    for j in range(per_groups):
        rank, slot = places[j]
        parent = recv[rank, slot]
        wider = jnp.dot(
            jnp.concatenate(split3(parent), axis=1), table_col[...], preferred_element_type=jnp.float32
        )
        child = jnp.dot(
            table_row[...], jnp.concatenate(split3(wider), axis=0), preferred_element_type=jnp.float32
        )
        for t in range(span // LANES):
            here = pl.ds(EDGE + j // groups_y * span, span)
            grid[3, j % groups_y * (span // LANES) + t, here, :] = child[:, t * LANES : (t + 1) * LANES]

    def first_half(tiles, start, total):
        def body(here, at, step):
            for i, of_v, mid in laplace(near(grid.at[3], at, step), step, tiles, ring):
                coef = grid[0, i, here, :]
                moment[i, here, :] = grid[1, i, here, :] * of_v - coef * mid
                rest[i, here, :] = grid[2, i, here, :] - (
                    mid * lap_u[i, here, :] - coef * of_v
                )

        sweep_rows(body, start, total)

    def second_half(tiles, start, total, store):
        def body(here, at, step):
            for i, of_m, _ in laplace(near(moment, at, step), step, tiles, ring):
                store(
                    at, step, here, i,
                    grid[3, i, here, :] + weight[i, here, :] * (rest[i, here, :] - of_m),
                )

        sweep_rows(body, start, total)

    field_copies = exchange(3, 1, 1)
    inside(first_half)
    settle(coef_copies, 0, 3)
    beside(coefficients)
    settle(field_copies, 3, 1)
    beside(first_half)

    def keep_field(at, step, here, i, value):
        grid[3, i, here, :] = value

    def keep_result(at, step, here, i, value):
        result[i, pl.ds(pl.multiple_of(at - EDGE, 8), step), :] = value

    for sweep in range(SWEEPS):
        if sweep:
            first_half(whole, EDGE - HALO, rows + 2 * HALO)
        if sweep < SWEEPS - 1:
            second_half(whole, EDGE - HALO, rows + 2 * HALO, keep_field)
            clear_outside()
    piece = rows // PIECES
    stores = []
    for p in range(PIECES):
        second_half(whole[:-1], EDGE + p * piece, piece, keep_result)
        part = pl.ds(p * piece, piece)
        for i in range(tiles):
            copy = pltpu.make_async_copy(
                result.at[i, part, :],
                out_hbm.at[part, pl.ds(i * LANES, LANES)],
                out_sem.at[p * tiles + i],
            )
            copy.start()
            stores.append(copy)
    for copy in stores:
        copy.wait()


def local(old_field, old_level, new_source, stretch_coef, bend_coef, load_field):
    wide_count = lax.axis_size("wide")
    narrow_count = lax.axis_size("narrow")
    groups_x, groups_y = new_source.shape
    per_device, side, _ = old_field.shape
    rows, cols = stretch_coef.shape
    used = groups_x * groups_y + per_device
    length = -(-used // LANES) * LANES
    tiles = cols // LANES
    full = (tiles + 1, rows + 2 * EDGE, LANES)
    chunk = rows * SLOT // LANES
    span = 2 * side
    f32 = jnp.float32
    dma = pltpu.SemaphoreType.DMA
    return pl.pallas_call(
        functools.partial(kernel, wide_count, narrow_count, groups_x, groups_y),
        out_shape=jax.ShapeDtypeStruct((rows, cols), f32),
        in_specs=[pl.BlockSpec(memory_space=pltpu.SMEM)] * 2 + [pl.BlockSpec(memory_space=pl.ANY)] * 4,
        out_specs=pl.BlockSpec(memory_space=pl.ANY),
        scratch_shapes=[
            pltpu.VMEM(old_field.shape, f32),
            pltpu.VMEM((wide_count, 1, length), jnp.int32),
            pltpu.SMEM((wide_count, 1, length), jnp.int32),
            pltpu.VMEM((wide_count, CAPACITY, side, side), f32),
            pltpu.VMEM((wide_count, CAPACITY, side, side), f32),
            pltpu.VMEM((4,) + full, f32),
            pltpu.VMEM(full, f32),
            pltpu.VMEM(full, f32),
            pltpu.VMEM(full, f32),
            pltpu.VMEM(full, f32),
            pltpu.VMEM((2, 4, chunk, LANES), f32),
            pltpu.VMEM((2, 4, chunk, LANES), f32),
            pltpu.VMEM((4, 4, HALO, LANES), f32),
            pltpu.VMEM((span, 3 * side), jnp.bfloat16),
            pltpu.VMEM((3 * side, span), jnp.bfloat16),
            pltpu.VMEM((tiles, rows, LANES), f32),
            pltpu.VMEM((1, length), jnp.int32),
            dma((1 + 3 * tiles,)),
            dma((wide_count,)),
            dma((wide_count,)),
            dma,
            dma((wide_count,)),
            dma((wide_count,)),
            dma((2, 8)),
            dma((2, 8)),
            dma((PIECES * tiles,)),
        ],
        compiler_params=pltpu.CompilerParams(
            collective_id=0, has_side_effects=True, vmem_limit_bytes=52 * 1024 * 1024
        ),
    )(new_source, old_level, old_field, stretch_coef, bend_coef, load_field)


def solution(mesh):
    return jax.shard_map(
        local,
        mesh=mesh,
        in_specs=(
            P(("wide", "narrow"), None, None),
            P(("wide", "narrow")),
            P("wide", "narrow"),
            P("wide", "narrow"),
            P("wide", "narrow"),
            P("wide", "narrow"),
        ),
        out_specs=P("wide", "narrow"),
        check_vma=False,
    )
```
